32 devices in a mesh: doc: 8 (over z, x), fsdp: 4 (over y, core).
Axes of the slice: x: 2, y: 2, z: 4, core: 2. Of those that a mesh axis runs over, the one named last changes fastest.
Arguments:
- activations: bfloat16 [128, 256, 8192], P('doc', None, 'fsdp'), may hold values from -6 to 6
- cotangents: bfloat16 [128, 256, 8192], P('doc', None, 'fsdp'), may hold values from -6 to 6
- adapter_down_matrix: bfloat16 [8192, 128], P('fsdp'), may hold values from -0.0625 to 0.0625
- targets: bfloat16 [512, 2048], P('fsdp', 'doc'), may hold values from -0.125 to 0.125
- projection_sign_seed: int32 [1], replicated, may hold values from 0 to 999999
Outputs:
- feature_gram: float32 [2048, 2048], P('doc', 'fsdp')
- scores: float32 [128, 512], P('doc', 'fsdp')
The draws below stay inside these ranges and needn't reach their ends.
All inputs are finite; a program needn't handle non-finite values.
Results may differ from the reference program's by a relative error of at most 0.025.
Values may be sent and summed in bfloat16 or wider, within the bound.
A program may use at most 128 MiB of HBM per device.

```python
import math
import jax
import jax.numpy as jnp
from jax import lax

MODEL_WIDTH = 8192
ADAPTER_RANK = 128
PROJECTED_DIMS = 2048
SEQ = 256
NDOCS = 128
NTGT = 512


def shard_levels(own_key, shape, cuts, least, top_value):
    gain, own = 1.0, jax.random.fold_in(own_key, 6)
    for dim, parts in cuts:
        draws = jnp.exp(jax.random.uniform(jax.random.fold_in(own, dim), (parts,), jnp.float32, least / len(cuts), top_value / len(cuts)))
        gain = gain * jnp.repeat(draws, shape[dim] // parts).reshape([-1 if axis == dim else 1 for axis in range(len(shape))])
    return gain


def bell_draw(own_key, extent, deviation, reach, cuts=(), held_as=jnp.bfloat16):
    entries = jax.random.normal(own_key, extent, jnp.float32) * deviation
    if len(cuts) > 0:
        entries = shard_levels(own_key, extent, cuts, -0.22, 0.18) * entries
    return jnp.clip(entries, min=-reach, max=reach).astype(held_as)


def setup_inputs(seed: int = 0) -> dict:
    seeds = jax.random.split(jax.random.key(seed), 6)
    return {
        "activations": bell_draw(seeds[0], (NDOCS, SEQ, MODEL_WIDTH), 1.0, 6.0, ((0, 8), (2, 4))),
        "cotangents": bell_draw(seeds[1], (NDOCS, SEQ, MODEL_WIDTH), 1.0, 6.0, ((0, 8), (2, 4))),
        "adapter_down_matrix": bell_draw(seeds[2], (MODEL_WIDTH, ADAPTER_RANK), MODEL_WIDTH ** -0.5, 0.0625, ((0, 4),)),
        "targets": bell_draw(seeds[3], (NTGT, PROJECTED_DIMS), PROJECTED_DIMS ** -0.5, 0.125, ((0, 4), (1, 8))),
        "projection_sign_seed": jax.random.randint(seeds[4], (1,), 0, 1000000).astype(jnp.int32),
    }


norm_eps = 1e-06

def sign_table(param_ids, column_ids, seed_value):
    hashed = param_ids[:, None] * -1640531535 + column_ids[None, :] * 668265263 + seed_value
    hashed = hashed ^ hashed >> 15 & 131071
    hashed = hashed * -2048144789
    hashed = hashed ^ hashed >> 13 & 524287
    hashed = hashed * -1028477387
    hashed = hashed ^ hashed >> 16 & 65535
    low_bit = hashed >> 7 & 1
    return (1 - 2 * low_bit).astype(jnp.bfloat16)

def reference(activations, cotangents, adapter_down_matrix, targets, projection_sign_seed):
    document_total, sequence_length, complete_width = activations.shape
    adapter_rank = adapter_down_matrix.shape[1]
    flattened_tokens = activations.reshape(document_total * sequence_length, complete_width)
    reduced_rank_rows = jnp.dot(flattened_tokens, adapter_down_matrix, preferred_element_type=jnp.float32)
    reduced_rank_rows = reduced_rank_rows.astype(jnp.bfloat16).reshape(document_total, sequence_length, adapter_rank)

    def one_doc(doc_pair):
        low_doc, cot_doc = doc_pair
        return jnp.dot(low_doc.T, cot_doc, preferred_element_type=jnp.float32).astype(jnp.bfloat16)
    document_gradients = lax.map(one_doc, (reduced_rank_rows, cotangents))
    seed_value = projection_sign_seed[0]
    column_ids = jnp.arange(PROJECTED_DIMS, dtype=jnp.int32)

    def append_row(running, row_index):
        grads_row = lax.dynamic_index_in_dim(document_gradients, row_index, 1, keepdims=False)
        param_ids = row_index * complete_width + jnp.arange(complete_width, dtype=jnp.int32)
        sign_rows = sign_table(param_ids, column_ids, seed_value)
        return (running + jnp.dot(grads_row, sign_rows, preferred_element_type=jnp.float32), None)
    projected_features, unused_item = lax.scan(append_row, jnp.zeros((document_total, PROJECTED_DIMS), jnp.float32), jnp.arange(adapter_rank, dtype=jnp.int32))
    gradient_scale = 1.0 / math.sqrt(adapter_rank * complete_width * sequence_length)
    features = (projected_features * gradient_scale).astype(jnp.bfloat16)
    raw_scores = jnp.dot(features, targets.T, preferred_element_type=jnp.float32)
    energy = lax.optimization_barrier(jnp.sum(jnp.square(features.astype(jnp.float32)), axis=1))
    inverse_rms = lax.rsqrt(energy / PROJECTED_DIMS + norm_eps)
    scores = raw_scores * inverse_rms[:, None]
    feature_gram = lax.dot_general(features, features, (((0,), (0,)), ((), ())), preferred_element_type=jnp.float32) / document_total
    return (feature_gram, scores)
```

```python
import functools
import math

import jax
import jax.numpy as jnp
from jax import lax
from jax.experimental import pallas as pl
from jax.experimental.pallas import tpu as pltpu
from jax.sharding import PartitionSpec as P

PROJECTED_DIMS = 2048
MESH = pl.DeviceIdType.MESH
norm_eps = 1e-06
ROWS = 32
AHEAD = 4


def wrap(value):
    return jnp.int32((value + 2**31) % 2**32 - 2**31)


def signs(hashed):
    hashed = hashed ^ lax.shift_right_logical(hashed, 15)
    hashed = hashed * wrap(-2048144789)
    hashed = hashed ^ lax.shift_right_logical(hashed, 13)
    hashed = hashed * wrap(-1028477387 * 256)
    hashed = hashed ^ (hashed << 16)
    return jnp.where(hashed < 0, jnp.bfloat16(-1), jnp.bfloat16(1))


def greet(groups):
    barrier = pltpu.get_barrier_semaphore()
    count = 0
    for axis, size in groups:
        me = lax.axis_index(axis)
        for k in range(1, size):
            pl.semaphore_signal(
                barrier, inc=1, device_id={axis: lax.rem(me + k, size)}, device_id_type=MESH
            )
            count += 1
    pl.semaphore_wait(barrier, count)


def exchange(axis, size, source, target, send, recv):
    me = lax.axis_index(axis)
    copies = []
    for k in range(1, size):
        peer = lax.rem(me + k, size)
        copies.append(
            pltpu.make_async_remote_copy(
                src_ref=source(peer),
                dst_ref=target(me),
                send_sem=send.at[k],
                recv_sem=recv.at[k],
                device_id={axis: peer},
                device_id_type=MESH,
            )
        )
    return copies


def run(copies):
    for copy in copies:
        copy.start()
    for copy in copies:
        copy.wait()


def rank_kernel(shards, part_ref, out_ref, got, s0, r0, s1, r1):
    me = lax.axis_index("fsdp")
    rows = part_ref.shape[0] // shards

    def block(i):
        return pl.ds(pl.multiple_of(i * rows, rows), rows)

    greet([("fsdp", shards)])
    run(exchange("fsdp", shards, lambda p: part_ref.at[block(p)], lambda m: got.at[m], s0, r0))
    total = part_ref[block(me), :].astype(jnp.float32)
    for k in range(1, shards):
        total += got[lax.rem(me + k, shards)].astype(jnp.float32)
    out_ref[block(me), :] = total.astype(jnp.bfloat16)
    run(exchange("fsdp", shards, lambda p: out_ref.at[block(me)], lambda m: out_ref.at[block(m)], s1, r1))


def project_kernel(
    nd, nf, scale, seed_ref, grads_ref, tin_ref, gram_ref, scores_ref,
    landed, base, total, targets, outgoing, got_a, mid, got_b, feats,
    gs, gr, own_sem, ts, tr, s0, r0, s1, r1, s2, r2, s3, r3,
):
    doc, shard = lax.axis_index("doc"), lax.axis_index("fsdp")
    ranks, docs, width = grads_ref.shape
    steps = ranks // nd
    complete_width = width * nf
    rows_len, cols_len = PROJECTED_DIMS // nd, PROJECTED_DIMS // nf
    everyone = docs * nd
    kp = min(512, width)
    kc = 512

    def doc_rows(i):
        return pl.ds(pl.multiple_of(i * docs, docs), docs)

    def target_cols(i):
        return pl.ds(pl.multiple_of(i * rows_len, rows_len), rows_len)

    def grad_copy(s, k):
        peer = lax.rem(doc + k, nd)
        return pltpu.make_async_remote_copy(
            src_ref=grads_ref.at[peer * steps + s],
            dst_ref=landed.at[s, doc_rows(doc)],
            send_sem=gs.at[s, k],
            recv_sem=gr.at[s, k],
            device_id={"doc": peer},
            device_id_type=MESH,
        )

    def own_copy(s):
        return pltpu.make_async_copy(
            grads_ref.at[doc * steps + s], landed.at[s, doc_rows(doc)], own_sem.at[s]
        )

    def send(s, carry):
        def one(k, c):
            grad_copy(s, k).start()
            return c

        lax.fori_loop(1, nd, one, 0)
        own_copy(s).start()
        return carry

    greet([("doc", nd), ("fsdp", nf)])
    ahead = min(AHEAD, steps)
    lax.fori_loop(0, ahead, send, 0)
    target_copies = exchange("doc", nd, lambda p: tin_ref, lambda m: targets.at[:, target_cols(m)], ts, tr)
    for copy in target_copies:
        copy.start()
    targets[:, target_cols(doc)] = tin_ref[...]

    column = lax.broadcasted_iota(jnp.int32, base.shape, 1)
    row = lax.broadcasted_iota(jnp.int32, base.shape, 0)
    base[...] = row * wrap(-1640531535) + column * wrap(668265263) + seed_ref[0]
    total[...] = jnp.zeros_like(total)

    def project(s, carry):
        @pl.when(s + ahead < steps)
        def _():
            send(s + ahead, 0)

        def one(k, c):
            grad_copy(s, k).wait()
            return c

        lax.fori_loop(1, nd, one, 0)
        own_copy(s).wait()

        def chunk(j, c):
            first = (doc * steps + s) * complete_width + shard * width + j * kp
            offset = first * wrap(-1640531535)
            left = landed[s, :, pl.ds(pl.multiple_of(j * kp, kp), kp)]
            for c0 in range(0, PROJECTED_DIMS, kc):
                held = base[:, c0 : c0 + kc] + offset
                table = jnp.concatenate(
                    [signs(held + wrap(q * ROWS * -1640531535)) for q in range(kp // ROWS)], 0
                )
                total[:, c0 : c0 + kc] += jnp.dot(left, table, preferred_element_type=jnp.float32)
            return c

        return lax.fori_loop(0, width // kp, chunk, carry)

    lax.fori_loop(0, steps, project, 0)

    for f in range(nf):
        outgoing[f] = total[:, f * cols_len : (f + 1) * cols_len].astype(jnp.bfloat16)
    run(exchange("fsdp", nf, lambda p: outgoing.at[p], lambda m: got_a.at[m], s0, r0))
    part = outgoing[shard].astype(jnp.float32)
    for k in range(1, nf):
        part += got_a[lax.rem(shard + k, nf)].astype(jnp.float32)
    mid[...] = part.astype(jnp.bfloat16)
    run(exchange("doc", nd, lambda p: mid.at[doc_rows(p)], lambda m: got_b.at[m], s1, r1))
    feature = mid[doc_rows(doc), :].astype(jnp.float32)
    for k in range(1, nd):
        feature += got_b[lax.rem(doc + k, nd)].astype(jnp.float32)
    feats[shard, doc_rows(doc), :] = (feature * scale).astype(jnp.bfloat16)
    run(
        exchange(
            "doc", nd, lambda p: feats.at[shard, doc_rows(doc)],
            lambda m: feats.at[shard, doc_rows(m)], s2, r2,
        )
    )
    run(exchange("fsdp", nf, lambda p: feats.at[shard], lambda m: feats.at[m], s3, r3))
    for copy in target_copies:
        copy.wait()

    per = cols_len // rows_len
    gram_rows = feats[doc // per, :, pl.ds(pl.multiple_of(doc % per * rows_len, rows_len), rows_len)]
    gram_ref[...] = lax.dot_general(
        gram_rows, feats[shard], (((0,), (0,)), ((), ())), preferred_element_type=jnp.float32
    ) / everyone
    raw = jnp.zeros(scores_ref.shape, jnp.float32)
    energy = jnp.zeros((docs, 1), jnp.float32)
    for f in range(nf):
        mine = feats[f, doc_rows(doc), :]
        raw += lax.dot_general(
            mine, targets[:, f * cols_len : (f + 1) * cols_len],
            (((1,), (1,)), ((), ())), preferred_element_type=jnp.float32,
        )
        energy += jnp.sum(jnp.square(mine.astype(jnp.float32)), axis=1, keepdims=True)
    scores_ref[...] = raw * lax.rsqrt(energy / PROJECTED_DIMS + norm_eps)


def body(activations, cotangents, adapter_down_matrix, targets, projection_sign_seed):
    nd, nf = lax.axis_size("doc"), lax.axis_size("fsdp")
    docs, tokens, width = activations.shape
    rank = adapter_down_matrix.shape[1]
    scale = 1.0 / math.sqrt(rank * width * nf * tokens)
    steps = rank // nd
    rows_len, cols_len = PROJECTED_DIMS // nd, PROJECTED_DIMS // nf
    vmem = pl.BlockSpec(memory_space=pltpu.VMEM)
    bf16, f32 = jnp.bfloat16, jnp.float32
    dma = pltpu.SemaphoreType.DMA

    part = jnp.dot(
        activations.reshape(docs * tokens, width), adapter_down_matrix, preferred_element_type=f32
    ).astype(bf16)
    low = pl.pallas_call(
        functools.partial(rank_kernel, nf),
        out_shape=jax.ShapeDtypeStruct((docs * tokens, rank), bf16),
        in_specs=[vmem],
        out_specs=vmem,
        scratch_shapes=[pltpu.VMEM((nf, docs * tokens // nf, rank), bf16)] + [dma((nf,))] * 4,
        compiler_params=pltpu.CompilerParams(
            collective_id=0, has_side_effects=True, vmem_limit_bytes=32 * 2**20
        ),
    )(part)
    grads = jnp.einsum(
        "esr,esc->rec", low.reshape(docs, tokens, rank), cotangents, preferred_element_type=f32
    ).astype(bf16)
    return pl.pallas_call(
        functools.partial(project_kernel, nd, nf, scale),
        out_shape=(
            jax.ShapeDtypeStruct((rows_len, cols_len), f32),
            jax.ShapeDtypeStruct((docs, targets.shape[0]), f32),
        ),
        in_specs=[
            pl.BlockSpec(memory_space=pltpu.SMEM), pl.BlockSpec(memory_space=pl.ANY), vmem,
        ],
        out_specs=(vmem, vmem),
        scratch_shapes=[
            pltpu.VMEM((steps, docs * nd, width), bf16),
            pltpu.VMEM((ROWS, PROJECTED_DIMS), jnp.int32),
            pltpu.VMEM((docs * nd, PROJECTED_DIMS), f32),
            pltpu.VMEM((targets.shape[0], PROJECTED_DIMS), bf16),
            pltpu.VMEM((nf, docs * nd, cols_len), bf16),
            pltpu.VMEM((nf, docs * nd, cols_len), bf16),
            pltpu.VMEM((docs * nd, cols_len), bf16),
            pltpu.VMEM((nd, docs, cols_len), bf16),
            pltpu.VMEM((nf, docs * nd, cols_len), bf16),
            dma((steps, nd)), dma((steps, nd)), dma((steps,)),
            dma((nd,)), dma((nd,)), dma((nf,)), dma((nf,)),
            dma((nd,)), dma((nd,)), dma((nd,)), dma((nd,)), dma((nf,)), dma((nf,)),
        ],
        compiler_params=pltpu.CompilerParams(
            collective_id=1, has_side_effects=True, vmem_limit_bytes=56 * 2**20
        ),
    )(projection_sign_seed, grads, targets)


def solution(mesh):
    in_specs = (
        P("doc", None, "fsdp"),
        P("doc", None, "fsdp"),
        P("fsdp", None),
        P("fsdp", "doc"),
        P(),
    )
    out_specs = (P("doc", "fsdp"), P("doc", "fsdp"))
    return jax.shard_map(body, mesh=mesh, in_specs=in_specs, out_specs=out_specs, check_vma=False)
```

```python
import functools
import math

import jax
import jax.numpy as jnp
from jax import lax
from jax.experimental import pallas as pl
from jax.experimental.pallas import tpu as pltpu
from jax.sharding import PartitionSpec as P

PROJECTED_DIMS = 2048
MESH = pl.DeviceIdType.MESH
norm_eps = 1e-06
ROWS = 32
AHEAD = 4
HALVED = 4


def wrap(value):
    return jnp.int32((value + 2**31) % 2**32 - 2**31)


def signs(hashed):
    hashed = hashed ^ lax.shift_right_logical(hashed, 15)
    hashed = hashed * wrap(-2048144789)
    hashed = hashed ^ lax.shift_right_logical(hashed, 13)
    hashed = hashed * wrap(-1028477387 * 256)
    hashed = hashed ^ (hashed << 16)
    return jnp.where(hashed < 0, jnp.bfloat16(-1), jnp.bfloat16(1))


def greet(groups):
    barrier = pltpu.get_barrier_semaphore()
    count = 0
    for axis, size in groups:
        me = lax.axis_index(axis)
        for k in range(1, size):
            pl.semaphore_signal(
                barrier, inc=1, device_id={axis: lax.rem(me + k, size)}, device_id_type=MESH
            )
            count += 1
    pl.semaphore_wait(barrier, count)


def exchange(axis, size, source, target, send, recv):
    me = lax.axis_index(axis)
    copies = []
    for k in range(1, size):
        peer = lax.rem(me + k, size)
        copies.append(
            pltpu.make_async_remote_copy(
                src_ref=source(peer),
                dst_ref=target(me),
                send_sem=send.at[k],
                recv_sem=recv.at[k],
                device_id={axis: peer},
                device_id_type=MESH,
            )
        )
    return copies


def run(copies):
    for copy in copies:
        copy.start()
    for copy in copies:
        copy.wait()


def rank_kernel(shards, part_ref, out_ref, got, s0, r0, s1, r1):
    me = lax.axis_index("fsdp")
    rows = part_ref.shape[0] // shards

    def block(i):
        return pl.ds(pl.multiple_of(i * rows, rows), rows)

    greet([("fsdp", shards)])
    run(exchange("fsdp", shards, lambda p: part_ref.at[block(p)], lambda m: got.at[m], s0, r0))
    total = part_ref[block(me), :].astype(jnp.float32)
    for k in range(1, shards):
        total += got[lax.rem(me + k, shards)].astype(jnp.float32)
    out_ref[block(me), :] = total.astype(jnp.bfloat16)
    run(exchange("fsdp", shards, lambda p: out_ref.at[block(me)], lambda m: out_ref.at[block(m)], s1, r1))


def project_kernel(
    nd, nf, scale, seed_ref, grads_ref, tin_ref, gram_ref, scores_ref,
    landed, near, base, total, targets, outgoing, got_a, mid, got_b, feats,
    gs, gr, own_sem, hs, hr, near_sem, ts, tr, s0, r0, s1, r1, s2, r2, s3, r3,
):
    doc, shard = lax.axis_index("doc"), lax.axis_index("fsdp")
    ranks, docs, width = grads_ref.shape
    half = nd // 2
    whole_ranks = ranks - ranks // HALVED
    steps, near_steps = whole_ranks // nd, (ranks - whole_ranks) // half
    side, place = doc // half, lax.rem(doc, half)
    near_docs = docs * half
    complete_width = width * nf
    rows_len, cols_len = PROJECTED_DIMS // nd, PROJECTED_DIMS // nf
    everyone = docs * nd
    kp = min(512, width)
    kc = 512

    def doc_rows(i):
        return pl.ds(pl.multiple_of(i * docs, docs), docs)

    def target_cols(i):
        return pl.ds(pl.multiple_of(i * rows_len, rows_len), rows_len)

    def grad_copy(s, k):
        peer = lax.rem(doc + k, nd)
        return pltpu.make_async_remote_copy(
            src_ref=grads_ref.at[peer * steps + s],
            dst_ref=landed.at[s, doc_rows(doc)],
            send_sem=gs.at[s, k],
            recv_sem=gr.at[s, k],
            device_id={"doc": peer},
            device_id_type=MESH,
        )

    def own_copy(s):
        return pltpu.make_async_copy(
            grads_ref.at[doc * steps + s], landed.at[s, doc_rows(doc)], own_sem.at[s]
        )

    def send(s, carry):
        def one(k, c):
            grad_copy(s, k).start()
            return c

        lax.fori_loop(1, nd, one, 0)
        own_copy(s).start()
        return carry

    def near_copy(s, k):
        peer = lax.rem(place + k, half)
        return pltpu.make_async_remote_copy(
            src_ref=grads_ref.at[whole_ranks + peer * near_steps + s],
            dst_ref=near.at[s, doc_rows(place)],
            send_sem=hs.at[s, k],
            recv_sem=hr.at[s, k],
            device_id={"doc": side * half + peer},
            device_id_type=MESH,
        )

    def near_own(s):
        return pltpu.make_async_copy(
            grads_ref.at[whole_ranks + place * near_steps + s],
            near.at[s, doc_rows(place)],
            near_sem.at[s],
        )

    def near_send(s, carry):
        def one(k, c):
            near_copy(s, k).start()
            return c

        lax.fori_loop(1, half, one, 0)
        near_own(s).start()
        return carry

    greet([("doc", nd), ("fsdp", nf)])
    ahead = min(AHEAD, steps)
    for i in range(ahead):
        lax.fori_loop(near_steps * i // ahead, near_steps * (i + 1) // ahead, near_send, 0)
        send(i, 0)
    target_copies = exchange("doc", nd, lambda p: tin_ref, lambda m: targets.at[:, target_cols(m)], ts, tr)
    for copy in target_copies:
        copy.start()
    targets[:, target_cols(doc)] = tin_ref[...]

    column = lax.broadcasted_iota(jnp.int32, base.shape, 1)
    row = lax.broadcasted_iota(jnp.int32, base.shape, 0)
    base[...] = row * wrap(-1640531535) + column * wrap(668265263) + seed_ref[0]
    total[...] = jnp.zeros_like(total)

    def multiply(block, rank, rows):
        def chunk(j, c):
            first = rank * complete_width + shard * width + j * kp
            offset = first * wrap(-1640531535)
            left = block[:, pl.ds(pl.multiple_of(j * kp, kp), kp)]
            for c0 in range(0, PROJECTED_DIMS, kc):
                held = base[:, c0 : c0 + kc] + offset
                table = jnp.concatenate(
                    [signs(held + wrap(q * ROWS * -1640531535)) for q in range(kp // ROWS)], 0
                )
                total[rows, c0 : c0 + kc] += jnp.dot(
                    left, table, preferred_element_type=jnp.float32
                )
            return c

        lax.fori_loop(0, width // kp, chunk, 0)

    near_rows = pl.ds(pl.multiple_of(side * near_docs, near_docs), near_docs)

    def project_near(s, carry):
        @pl.when(s + ahead < steps)
        def _():
            send(s + ahead, 0)

        def one(k, c):
            near_copy(s, k).wait()
            return c

        lax.fori_loop(1, half, one, 0)
        near_own(s).wait()
        multiply(near.at[s], whole_ranks + place * near_steps + s, near_rows)
        return carry

    lax.fori_loop(0, near_steps, project_near, 0)

    def project(s, carry):
        @pl.when(s + ahead + near_steps < steps)
        def _():
            send(s + ahead + near_steps, 0)

        def one(k, c):
            grad_copy(s, k).wait()
            return c

        lax.fori_loop(1, nd, one, 0)
        own_copy(s).wait()
        multiply(landed.at[s], doc * steps + s, slice(None))
        return carry

    lax.fori_loop(0, steps, project, 0)

    for f in range(nf):
        outgoing[f] = total[:, f * cols_len : (f + 1) * cols_len].astype(jnp.bfloat16)
    run(exchange("fsdp", nf, lambda p: outgoing.at[p], lambda m: got_a.at[m], s0, r0))
    part = outgoing[shard].astype(jnp.float32)
    for k in range(1, nf):
        part += got_a[lax.rem(shard + k, nf)].astype(jnp.float32)
    mid[...] = part.astype(jnp.bfloat16)
    run(exchange("doc", nd, lambda p: mid.at[doc_rows(p)], lambda m: got_b.at[m], s1, r1))
    feature = mid[doc_rows(doc), :].astype(jnp.float32)
    for k in range(1, nd):
        feature += got_b[lax.rem(doc + k, nd)].astype(jnp.float32)
    feats[shard, doc_rows(doc), :] = (feature * scale).astype(jnp.bfloat16)
    run(
        exchange(
            "doc", nd, lambda p: feats.at[shard, doc_rows(doc)],
            lambda m: feats.at[shard, doc_rows(m)], s2, r2,
        )
    )
    run(exchange("fsdp", nf, lambda p: feats.at[shard], lambda m: feats.at[m], s3, r3))
    for copy in target_copies:
        copy.wait()

    per = cols_len // rows_len
    gram_rows = feats[doc // per, :, pl.ds(pl.multiple_of(doc % per * rows_len, rows_len), rows_len)]
    gram_ref[...] = lax.dot_general(
        gram_rows, feats[shard], (((0,), (0,)), ((), ())), preferred_element_type=jnp.float32
    ) / everyone
    raw = jnp.zeros(scores_ref.shape, jnp.float32)
    energy = jnp.zeros((docs, 1), jnp.float32)
    for f in range(nf):
        mine = feats[f, doc_rows(doc), :]
        raw += lax.dot_general(
            mine, targets[:, f * cols_len : (f + 1) * cols_len],
            (((1,), (1,)), ((), ())), preferred_element_type=jnp.float32,
        )
        energy += jnp.sum(jnp.square(mine.astype(jnp.float32)), axis=1, keepdims=True)
    scores_ref[...] = raw * lax.rsqrt(energy / PROJECTED_DIMS + norm_eps)


def body(activations, cotangents, adapter_down_matrix, targets, projection_sign_seed):
    nd, nf = lax.axis_size("doc"), lax.axis_size("fsdp")
    docs, tokens, width = activations.shape
    rank = adapter_down_matrix.shape[1]
    scale = 1.0 / math.sqrt(rank * width * nf * tokens)
    near_steps = rank // HALVED // (nd // 2)
    steps = (rank - rank // HALVED) // nd
    rows_len, cols_len = PROJECTED_DIMS // nd, PROJECTED_DIMS // nf
    vmem = pl.BlockSpec(memory_space=pltpu.VMEM)
    bf16, f32 = jnp.bfloat16, jnp.float32
    dma = pltpu.SemaphoreType.DMA

    part = jnp.dot(
        activations.reshape(docs * tokens, width), adapter_down_matrix, preferred_element_type=f32
    ).astype(bf16)
    low = pl.pallas_call(
        functools.partial(rank_kernel, nf),
        out_shape=jax.ShapeDtypeStruct((docs * tokens, rank), bf16),
        in_specs=[vmem],
        out_specs=vmem,
        scratch_shapes=[pltpu.VMEM((nf, docs * tokens // nf, rank), bf16)] + [dma((nf,))] * 4,
        compiler_params=pltpu.CompilerParams(
            collective_id=0, has_side_effects=True, vmem_limit_bytes=32 * 2**20
        ),
    )(part)
    grads = jnp.einsum(
        "esr,esc->rec", low.reshape(docs, tokens, rank), cotangents, preferred_element_type=f32
    ).astype(bf16)
    return pl.pallas_call(
        functools.partial(project_kernel, nd, nf, scale),
        out_shape=(
            jax.ShapeDtypeStruct((rows_len, cols_len), f32),
            jax.ShapeDtypeStruct((docs, targets.shape[0]), f32),
        ),
        in_specs=[
            pl.BlockSpec(memory_space=pltpu.SMEM), pl.BlockSpec(memory_space=pl.ANY), vmem,
        ],
        out_specs=(vmem, vmem),
        scratch_shapes=[
            pltpu.VMEM((steps, docs * nd, width), bf16),
            pltpu.VMEM((near_steps, docs * nd // 2, width), bf16),
            pltpu.VMEM((ROWS, PROJECTED_DIMS), jnp.int32),
            pltpu.VMEM((docs * nd, PROJECTED_DIMS), f32),
            pltpu.VMEM((targets.shape[0], PROJECTED_DIMS), bf16),
            pltpu.VMEM((nf, docs * nd, cols_len), bf16),
            pltpu.VMEM((nf, docs * nd, cols_len), bf16),
            pltpu.VMEM((docs * nd, cols_len), bf16),
            pltpu.VMEM((nd, docs, cols_len), bf16),
            pltpu.VMEM((nf, docs * nd, cols_len), bf16),
            dma((steps, nd)), dma((steps, nd)), dma((steps,)),
            dma((near_steps, nd // 2)), dma((near_steps, nd // 2)), dma((near_steps,)),
            dma((nd,)), dma((nd,)), dma((nf,)), dma((nf,)),
            dma((nd,)), dma((nd,)), dma((nd,)), dma((nd,)), dma((nf,)), dma((nf,)),
        ],
        compiler_params=pltpu.CompilerParams(
            collective_id=1, has_side_effects=True, vmem_limit_bytes=56 * 2**20
        ),
    )(projection_sign_seed, grads, targets)


def solution(mesh):
    in_specs = (
        P("doc", None, "fsdp"),
        P("doc", None, "fsdp"),
        P("fsdp", None),
        P("fsdp", "doc"),
        P(),
    )
    out_specs = (P("doc", "fsdp"), P("doc", "fsdp"))
    return jax.shard_map(body, mesh=mesh, in_specs=in_specs, out_specs=out_specs, check_vma=False)
```

```python
import functools
import math

import jax
import jax.numpy as jnp
from jax import lax
from jax.experimental import pallas as pl
from jax.experimental.pallas import tpu as pltpu
from jax.sharding import PartitionSpec as P

PROJECTED_DIMS = 2048
MESH = pl.DeviceIdType.MESH
norm_eps = 1e-06
ROWS = 32
AHEAD = 4
HALVED = 4


def wrap(value):
    return jnp.int32((value + 2**31) % 2**32 - 2**31)


def signs(hashed):
    hashed = hashed ^ lax.shift_right_logical(hashed, 15)
    hashed = hashed * wrap(-2048144789)
    hashed = hashed ^ lax.shift_right_logical(hashed, 13)
    hashed = hashed * wrap(-1028477387 * 256)
    hashed = hashed ^ (hashed << 16)
    return jnp.where(hashed < 0, jnp.bfloat16(-1), jnp.bfloat16(1))


def greet(groups):
    barrier = pltpu.get_barrier_semaphore()
    count = 0
    for axis, size in groups:
        me = lax.axis_index(axis)
        for k in range(1, size):
            pl.semaphore_signal(
                barrier, inc=1, device_id={axis: lax.rem(me + k, size)}, device_id_type=MESH
            )
            count += 1
    pl.semaphore_wait(barrier, count)


def exchange(axis, size, source, target, send, recv):
    me = lax.axis_index(axis)
    copies = []
    for k in range(1, size):
        peer = lax.rem(me + k, size)
        copies.append(
            pltpu.make_async_remote_copy(
                src_ref=source(peer),
                dst_ref=target(me),
                send_sem=send.at[k],
                recv_sem=recv.at[k],
                device_id={axis: peer},
                device_id_type=MESH,
            )
        )
    return copies


def run(copies):
    for copy in copies:
        copy.start()
    for copy in copies:
        copy.wait()


def rank_kernel(shards, part_ref, out_ref, got, s0, r0, s1, r1):
    me = lax.axis_index("fsdp")
    rows = part_ref.shape[0] // shards

    def block(i):
        return pl.ds(pl.multiple_of(i * rows, rows), rows)

    greet([("fsdp", shards)])
    run(exchange("fsdp", shards, lambda p: part_ref.at[block(p)], lambda m: got.at[m], s0, r0))
    total = part_ref[block(me), :].astype(jnp.float32)
    for k in range(1, shards):
        total += got[lax.rem(me + k, shards)].astype(jnp.float32)
    out_ref[block(me), :] = total.astype(jnp.bfloat16)
    run(exchange("fsdp", shards, lambda p: out_ref.at[block(me)], lambda m: out_ref.at[block(m)], s1, r1))


def grads_kernel(low_ref, cot_ref, out_ref, held):
    for e in range(low_ref.shape[0]):
        held[:, e, :] = lax.dot_general(
            low_ref[e], cot_ref[e], (((0,), (0,)), ((), ())), preferred_element_type=jnp.float32
        )
    out_ref[...] = held[...].astype(jnp.bfloat16)


def project_kernel(
    nd, nf, scale, seed_ref, grads_ref, tin_ref, gram_ref, scores_ref,
    landed, near, base, total, targets, outgoing, got_a, mid, got_b, feats,
    gs, gr, own_sem, hs, hr, near_sem, ts, tr, s0, r0, s1, r1, s2, r2, s3, r3,
):
    doc, shard = lax.axis_index("doc"), lax.axis_index("fsdp")
    ranks, docs, width = grads_ref.shape
    half = nd // 2
    whole_ranks = ranks - ranks // HALVED
    steps, near_steps = whole_ranks // nd, (ranks - whole_ranks) // half
    side, place = doc // half, lax.rem(doc, half)
    near_docs = docs * half
    complete_width = width * nf
    rows_len, cols_len = PROJECTED_DIMS // nd, PROJECTED_DIMS // nf
    everyone = docs * nd
    kp = min(512, width)
    kc = 512

    def doc_rows(i):
        return pl.ds(pl.multiple_of(i * docs, docs), docs)

    def target_cols(i):
        return pl.ds(pl.multiple_of(i * rows_len, rows_len), rows_len)

    def grad_copy(s, k):
        peer = lax.rem(doc + k, nd)
        return pltpu.make_async_remote_copy(
            src_ref=grads_ref.at[peer * steps + s],
            dst_ref=landed.at[s, doc_rows(doc)],
            send_sem=gs.at[s, k],
            recv_sem=gr.at[s, k],
            device_id={"doc": peer},
            device_id_type=MESH,
        )

    def own_copy(s):
        return pltpu.make_async_copy(
            grads_ref.at[doc * steps + s], landed.at[s, doc_rows(doc)], own_sem.at[s]
        )

    def send(s, carry):
        def one(k, c):
            grad_copy(s, k).start()
            return c

        lax.fori_loop(1, nd, one, 0)
        own_copy(s).start()
        return carry

    def near_copy(s, k):
        peer = lax.rem(place + k, half)
        return pltpu.make_async_remote_copy(
            src_ref=grads_ref.at[whole_ranks + peer * near_steps + s],
            dst_ref=near.at[s, doc_rows(place)],
            send_sem=hs.at[s, k],
            recv_sem=hr.at[s, k],
            device_id={"doc": side * half + peer},
            device_id_type=MESH,
        )

    def near_own(s):
        return pltpu.make_async_copy(
            grads_ref.at[whole_ranks + place * near_steps + s],
            near.at[s, doc_rows(place)],
            near_sem.at[s],
        )

    def near_send(s, carry):
        def one(k, c):
            near_copy(s, k).start()
            return c

        lax.fori_loop(1, half, one, 0)
        near_own(s).start()
        return carry

    greet([("doc", nd), ("fsdp", nf)])
    ahead = min(AHEAD, steps)
    for i in range(ahead):
        lax.fori_loop(near_steps * i // ahead, near_steps * (i + 1) // ahead, near_send, 0)
        send(i, 0)
    target_copies = exchange("doc", nd, lambda p: tin_ref, lambda m: targets.at[:, target_cols(m)], ts, tr)
    for copy in target_copies:
        copy.start()
    targets[:, target_cols(doc)] = tin_ref[...]

    column = lax.broadcasted_iota(jnp.int32, base.shape, 1)
    row = lax.broadcasted_iota(jnp.int32, base.shape, 0)
    base[...] = row * wrap(-1640531535) + column * wrap(668265263) + seed_ref[0]
    total[...] = jnp.zeros_like(total)

    def multiply(block, rank, rows):
        def chunk(j, c):
            first = rank * complete_width + shard * width + j * kp
            offset = first * wrap(-1640531535)
            left = block[:, pl.ds(pl.multiple_of(j * kp, kp), kp)]
            for c0 in range(0, PROJECTED_DIMS, kc):
                held = base[:, c0 : c0 + kc] + offset
                table = jnp.concatenate(
                    [signs(held + wrap(q * ROWS * -1640531535)) for q in range(kp // ROWS)], 0
                )
                total[rows, c0 : c0 + kc] += jnp.dot(
                    left, table, preferred_element_type=jnp.float32
                )
            return c

        lax.fori_loop(0, width // kp, chunk, 0)

    near_rows = pl.ds(pl.multiple_of(side * near_docs, near_docs), near_docs)

    def project_near(s, carry):
        @pl.when(s + ahead < steps)
        def _():
            send(s + ahead, 0)

        def one(k, c):
            near_copy(s, k).wait()
            return c

        lax.fori_loop(1, half, one, 0)
        near_own(s).wait()
        multiply(near.at[s], whole_ranks + place * near_steps + s, near_rows)
        return carry

    lax.fori_loop(0, near_steps, project_near, 0)

    def project(s, carry):
        @pl.when(s + ahead + near_steps < steps)
        def _():
            send(s + ahead + near_steps, 0)

        def one(k, c):
            grad_copy(s, k).wait()
            return c

        lax.fori_loop(1, nd, one, 0)
        own_copy(s).wait()
        multiply(landed.at[s], doc * steps + s, slice(None))
        return carry

    lax.fori_loop(0, steps, project, 0)

    for f in range(nf):
        outgoing[f] = total[:, f * cols_len : (f + 1) * cols_len].astype(jnp.bfloat16)
    run(exchange("fsdp", nf, lambda p: outgoing.at[p], lambda m: got_a.at[m], s0, r0))
    part = outgoing[shard].astype(jnp.float32)
    for k in range(1, nf):
        part += got_a[lax.rem(shard + k, nf)].astype(jnp.float32)
    mid[...] = part.astype(jnp.bfloat16)
    run(exchange("doc", nd, lambda p: mid.at[doc_rows(p)], lambda m: got_b.at[m], s1, r1))
    feature = mid[doc_rows(doc), :].astype(jnp.float32)
    for k in range(1, nd):
        feature += got_b[lax.rem(doc + k, nd)].astype(jnp.float32)
    feats[shard, doc_rows(doc), :] = (feature * scale).astype(jnp.bfloat16)
    run(
        exchange(
            "doc", nd, lambda p: feats.at[shard, doc_rows(doc)],
            lambda m: feats.at[shard, doc_rows(m)], s2, r2,
        )
    )
    run(exchange("fsdp", nf, lambda p: feats.at[shard], lambda m: feats.at[m], s3, r3))
    for copy in target_copies:
        copy.wait()

    per = cols_len // rows_len
    gram_rows = feats[doc // per, :, pl.ds(pl.multiple_of(doc % per * rows_len, rows_len), rows_len)]
    gram_ref[...] = lax.dot_general(
        gram_rows, feats[shard], (((0,), (0,)), ((), ())), preferred_element_type=jnp.float32
    ) / everyone
    raw = jnp.zeros(scores_ref.shape, jnp.float32)
    energy = jnp.zeros((docs, 1), jnp.float32)
    for f in range(nf):
        mine = feats[f, doc_rows(doc), :]
        raw += lax.dot_general(
            mine, targets[:, f * cols_len : (f + 1) * cols_len],
            (((1,), (1,)), ((), ())), preferred_element_type=jnp.float32,
        )
        energy += jnp.sum(jnp.square(mine.astype(jnp.float32)), axis=1, keepdims=True)
    scores_ref[...] = raw * lax.rsqrt(energy / PROJECTED_DIMS + norm_eps)


def body(activations, cotangents, adapter_down_matrix, targets, projection_sign_seed):
    nd, nf = lax.axis_size("doc"), lax.axis_size("fsdp")
    docs, tokens, width = activations.shape
    rank = adapter_down_matrix.shape[1]
    scale = 1.0 / math.sqrt(rank * width * nf * tokens)
    near_steps = rank // HALVED // (nd // 2)
    steps = (rank - rank // HALVED) // nd
    rows_len, cols_len = PROJECTED_DIMS // nd, PROJECTED_DIMS // nf
    vmem = pl.BlockSpec(memory_space=pltpu.VMEM)
    bf16, f32 = jnp.bfloat16, jnp.float32
    dma = pltpu.SemaphoreType.DMA

    part = jnp.dot(
        activations.reshape(docs * tokens, width), adapter_down_matrix, preferred_element_type=f32
    ).astype(bf16)
    low = pl.pallas_call(
        functools.partial(rank_kernel, nf),
        out_shape=jax.ShapeDtypeStruct((docs * tokens, rank), bf16),
        in_specs=[vmem],
        out_specs=vmem,
        scratch_shapes=[pltpu.VMEM((nf, docs * tokens // nf, rank), bf16)] + [dma((nf,))] * 4,
        compiler_params=pltpu.CompilerParams(
            collective_id=0, has_side_effects=True, vmem_limit_bytes=32 * 2**20
        ),
    )(part)
    tile = min(512, width)
    grads = pl.pallas_call(
        grads_kernel,
        grid=(width // tile,),
        out_shape=jax.ShapeDtypeStruct((rank, docs, width), bf16),
        in_specs=[
            pl.BlockSpec((docs, tokens, rank), lambda j: (0, 0, 0)),
            pl.BlockSpec((docs, tokens, tile), lambda j: (0, 0, j)),
        ],
        out_specs=pl.BlockSpec((rank, docs, tile), lambda j: (0, 0, j)),
        scratch_shapes=[pltpu.VMEM((rank, docs, tile), f32)],
        compiler_params=pltpu.CompilerParams(vmem_limit_bytes=40 * 2**20),
    )(low.reshape(docs, tokens, rank), cotangents)
    return pl.pallas_call(
        functools.partial(project_kernel, nd, nf, scale),
        out_shape=(
            jax.ShapeDtypeStruct((rows_len, cols_len), f32),
            jax.ShapeDtypeStruct((docs, targets.shape[0]), f32),
        ),
        in_specs=[
            pl.BlockSpec(memory_space=pltpu.SMEM), pl.BlockSpec(memory_space=pl.ANY), vmem,
        ],
        out_specs=(vmem, vmem),
        scratch_shapes=[
            pltpu.VMEM((steps, docs * nd, width), bf16),
            pltpu.VMEM((near_steps, docs * nd // 2, width), bf16),
            pltpu.VMEM((ROWS, PROJECTED_DIMS), jnp.int32),
            pltpu.VMEM((docs * nd, PROJECTED_DIMS), f32),
            pltpu.VMEM((targets.shape[0], PROJECTED_DIMS), bf16),
            pltpu.VMEM((nf, docs * nd, cols_len), bf16),
            pltpu.VMEM((nf, docs * nd, cols_len), bf16),
            pltpu.VMEM((docs * nd, cols_len), bf16),
            pltpu.VMEM((nd, docs, cols_len), bf16),
            pltpu.VMEM((nf, docs * nd, cols_len), bf16),
            dma((steps, nd)), dma((steps, nd)), dma((steps,)),
            dma((near_steps, nd // 2)), dma((near_steps, nd // 2)), dma((near_steps,)),
            dma((nd,)), dma((nd,)), dma((nf,)), dma((nf,)),
            dma((nd,)), dma((nd,)), dma((nd,)), dma((nd,)), dma((nf,)), dma((nf,)),
        ],
        compiler_params=pltpu.CompilerParams(
            collective_id=1, has_side_effects=True, vmem_limit_bytes=56 * 2**20
        ),
    )(projection_sign_seed, grads, targets)


def solution(mesh):
    in_specs = (
        P("doc", None, "fsdp"),
        P("doc", None, "fsdp"),
        P("fsdp", None),
        P("fsdp", "doc"),
        P(),
    )
    out_specs = (P("doc", "fsdp"), P("doc", "fsdp"))
    return jax.shard_map(body, mesh=mesh, in_specs=in_specs, out_specs=out_specs, check_vma=False)
```
